768 devices in a mesh: fault: 192 (over z, y, core), off: 4 (over x).
Axes of the slice: x: 4, y: 8, z: 12, core: 2. Of those that a mesh axis runs over, the one named last changes fastest.
Arguments:
- modal_state: float32 [9, 56, 24576], P(None, None, ('fault', 'off')), may hold values from -6 to 6
- star_mats: float32 [3, 9, 9, 24576], P(None, None, None, ('fault', 'off')), may hold values from -2 to 2
- flux_local: float32 [4, 9, 9, 24576], P(None, None, None, ('fault', 'off')), may hold values from -1 to 1
- flux_nbr: float32 [4, 9, 9, 24576], P(None, None, None, ('fault', 'off')), may hold values from -1 to 1
- stiff_time: float32 [3, 56, 56], replicated, may hold values from -0.75 to 0.75
- stiff_vol: float32 [3, 56, 56], replicated, may hold values from -0.375 to 0.375
- flux_minus: float32 [4, 56, 56], replicated, may hold values from -0.375 to 0.375
- face_proj: float32 [4, 56, 21], replicated, may hold values from -0.75 to 0.75
- face_turn: float32 [3, 21, 21], replicated, may hold values from -1.25 to 1.25
- face_lift: float32 [4, 21, 56], replicated, may hold values from -0.625 to 0.625
- cluster: int32 [24576], P(('fault', 'off')), may hold values from 0 to 1, as said below
- send_elem: int32 [192, 4, 72], P('fault', 'off'), may hold values from 0 to 31
- send_face: int32 [192, 4, 72], P('fault', 'off'), may hold values from 0 to 3
- nbr_index: int32 [4, 24576], P(None, ('fault', 'off')), may hold values from 0 to 199, as said below
- orientation: int32 [4, 24576], P(None, ('fault', 'off')), may hold values from 0 to 2
- source_elem: int32 [16], replicated, may hold values from 0 to 24575
- source_term: float32 [16, 9, 56], replicated, may hold values from -6 to 6
Outputs:
- new_state: float32 [9, 56, 24576], P(None, None, ('fault', 'off'))
The draws below stay inside these ranges and needn't reach their ends.
Inputs may be any that keep to these rules, and one draw needn't show every extreme that they name: `cluster`: each device holds at most 16 fine elements, and some device exactly 16 in every draw. `nbr_index`: on each device, entries below 128 name the device's own face traces; every received entry 128 .. 199 is named by exactly one face of the device.
All inputs are finite; a program needn't handle non-finite values.
Results may differ from the reference program's by a relative error of at most 0.0003.
Values sent between devices are 32-bit elements; how exact they have to be, the bound alone decides.
A program may use at most 32 MiB of HBM per device.

```python
import math
import jax
import jax.numpy as jnp
from jax import lax

QUANT = 9
MODES = 56
FACE_MODES = 21
TERMS = 6
SOURCES = 16
E_DEV = 32
SF = 16
SO = 10
SLOTS = 72
FINE_MAX = 16
E_TOTAL = 24576
N_FAULT = 192
N_OFF = 4


def draw_cluster(key, part):
    blocks = E_TOTAL // E_DEV
    key_count, key_block, key_perm = jax.random.split(key, 3)
    counts = jax.random.randint(key_count, (blocks,), FINE_MAX // 4, FINE_MAX + 1)
    full_block = jax.random.randint(key_block, (), 0, blocks)
    counts = jnp.where(jnp.arange(blocks) == full_block, FINE_MAX, counts)
    block_keys = jax.random.split(key_perm, blocks)
    ranking = jax.vmap(lambda sub_key: jax.random.permutation(sub_key, E_DEV))(block_keys).astype(jnp.int32)
    marked = (ranking < counts[:, None]).astype(jnp.int32)
    return marked.reshape(E_TOTAL)


def draw_nbr_index(key, part):
    blocks = E_TOTAL // E_DEV
    local_count = 4 * E_DEV
    key_perm, key_pick = jax.random.split(key)
    block_keys = jax.random.split(key_perm, blocks)
    ranking = jax.vmap(lambda sub_key: jax.random.permutation(sub_key, local_count))(block_keys).astype(jnp.int32)
    picks = jax.random.randint(key_pick, (blocks, local_count), 0, local_count)
    chosen = jnp.where(ranking < SLOTS, local_count + ranking, picks).astype(jnp.int32)
    return chosen.reshape(blocks, 4, E_DEV).transpose(1, 0, 2).reshape(4, E_TOTAL)


def touch_ends(values, rng, low, top_value):
    longest = values.shape.index(max(values.shape))
    spots = []
    for shift in (0, 1):
        where = [jax.random.randint(jax.random.fold_in(rng, axis), (), 0, length) for axis, length in enumerate(values.shape)]
        where[longest] = (where[longest] + shift) % values.shape[longest]
        spots.append(tuple(where))
    return values.at[spots[0]].set(low).at[spots[1]].set(top_value)


def levels(key, dims, cuts, smallest, largest):
    def one(dim, blocks):
        steps = jax.random.uniform(jax.random.fold_in(jax.random.fold_in(key, 6), dim), (blocks,), jnp.float32, smallest / len(cuts), largest / len(cuts))
        return jnp.repeat(jnp.exp(steps), dims[dim] // blocks).reshape((-1,) + (1,) * (len(dims) - dim - 1))

    gain = one(*cuts[0])
    for cut in cuts[1:]:
        gain = gain * one(*cut)
    return gain


def scatter_about(key, shape, deviation, most, shards=(), dtype=jnp.bfloat16):
    gain = levels(key, shape, shards, -0.22, 0.18) if shards else 1.0
    values = jax.random.normal(key, shape, jnp.float32) * deviation * gain
    return jnp.minimum(jnp.maximum(values, -most), most).astype(dtype)


def setup_inputs(seed: int = 0) -> dict:
    key_list = jax.random.split(jax.random.key(seed), 18)
    return {
        "modal_state": scatter_about(key_list[0], (QUANT, MODES, E_TOTAL), 1.0, 6.0, ((2, 768),), jnp.float32),
        "star_mats": scatter_about(key_list[1], (3, QUANT, QUANT, E_TOTAL), QUANT ** -0.5, 2.0, ((3, 768),), jnp.float32),
        "flux_local": scatter_about(key_list[2], (4, QUANT, QUANT, E_TOTAL), (4 * QUANT) ** -0.5, 1.0, ((3, 768),), jnp.float32),
        "flux_nbr": scatter_about(key_list[3], (4, QUANT, QUANT, E_TOTAL), (4 * QUANT) ** -0.5, 1.0, ((3, 768),), jnp.float32),
        "stiff_time": scatter_about(key_list[4], (3, MODES, MODES), MODES ** -0.5, 0.75, (), jnp.float32),
        "stiff_vol": scatter_about(key_list[5], (3, MODES, MODES), (4 * MODES) ** -0.5, 0.375, (), jnp.float32),
        "flux_minus": scatter_about(key_list[6], (4, MODES, MODES), (4 * MODES) ** -0.5, 0.375, (), jnp.float32),
        "face_proj": scatter_about(key_list[7], (4, MODES, FACE_MODES), MODES ** -0.5, 0.75, (), jnp.float32),
        "face_turn": scatter_about(key_list[8], (3, FACE_MODES, FACE_MODES), FACE_MODES ** -0.5, 1.25, (), jnp.float32),
        "face_lift": scatter_about(key_list[9], (4, FACE_MODES, MODES), (4 * FACE_MODES) ** -0.5, 0.625, (), jnp.float32),
        "cluster": draw_cluster(jax.random.fold_in(key_list[17], 71), 0),
        "send_elem": touch_ends(jax.random.randint(key_list[11], (N_FAULT, N_OFF, SLOTS), 0, E_DEV), jax.random.fold_in(key_list[11], 1), 0, E_DEV - 1).astype(jnp.int32),
        "send_face": touch_ends(jax.random.randint(key_list[12], (N_FAULT, N_OFF, SLOTS), 0, 4), jax.random.fold_in(key_list[12], 1), 0, 3).astype(jnp.int32),
        "nbr_index": draw_nbr_index(jax.random.fold_in(key_list[17], 71), 0),
        "orientation": touch_ends(jax.random.randint(key_list[14], (4, E_TOTAL), 0, 3), jax.random.fold_in(key_list[14], 1), 0, 2).astype(jnp.int32),
        "source_elem": touch_ends(jax.random.randint(key_list[15], (SOURCES,), 0, E_TOTAL), jax.random.fold_in(key_list[15], 1), 0, E_TOTAL - 1).astype(jnp.int32),
        "source_term": scatter_about(key_list[16], (SOURCES, QUANT, MODES), 1.0, 6.0, (), jnp.float32),
    }


PRECISE = lax.Precision.HIGHEST
HALF_STEP = 0.5


def weights_over(start, finish):
    return [(finish ** (degree + 1) - start ** (degree + 1)) / math.factorial(degree + 1) for degree in range(TERMS)]


def derive(modal_in, star_mats, stiffness):
    stiffened = jnp.einsum('pme,dmn->dpne', modal_in, stiffness, precision=PRECISE)
    return jnp.einsum('dqpe,dpne->qne', star_mats, stiffened, precision=PRECISE)


def predict(modal_in, star_mats, stiff_time):
    series = [modal_in]
    for degree in range(1, TERMS):
        series.append(derive(series[-1], star_mats, stiff_time))
    return series


def integrate(series, weights):
    summed = weights[0] * series[0]
    for degree in range(1, TERMS):
        summed = summed + weights[degree] * series[degree]
    return summed


def traces(integral, face_proj):
    faced = jnp.einsum('qme,fmj->qjfe', integral, face_proj, precision=PRECISE)
    return faced.reshape(faced.shape[0], faced.shape[1], 4 * integral.shape[2])


def update(base_state, integral, neighbours, star_mats, flux_local, flux_nbr, stiff_vol, flux_minus, face_turn, face_lift, orientation):
    volume = derive(integral, star_mats, stiff_vol)
    face_flux = jnp.einsum('pme,fmn->fpne', integral, flux_minus, precision=PRECISE)
    local_part = jnp.einsum('fqpe,fpne->qne', flux_local, face_flux, precision=PRECISE)
    rotated = [jnp.einsum('qife,ij->qjfe', neighbours, face_turn[facing], precision=PRECISE) for facing in range(3)]
    facing_now = orientation[None, None]
    turned = jnp.where(facing_now == 0, rotated[0], jnp.where(facing_now == 1, rotated[1], rotated[2]))
    lifted = jnp.einsum('qjfe,fjn->fqne', turned, face_lift, precision=PRECISE)
    nbr_part = jnp.einsum('fqpe,fpne->qne', flux_nbr, lifted, precision=PRECISE)
    return base_state + volume + local_part + nbr_part


def receive(outgoing):
    blocks = outgoing.shape[0]
    quant, face_modes = outgoing.shape[1], outgoing.shape[2]
    grid = outgoing.reshape(N_FAULT, N_OFF, quant, face_modes, SLOTS)
    rim_slots = grid[..., :2 * SF]
    lower = jnp.roll(rim_slots, 1, axis=0)[..., SF:]
    upper = jnp.roll(rim_slots, -1, axis=0)[..., :SF]
    off_part = grid[..., 2 * SF:].reshape(N_FAULT, N_OFF, quant, face_modes, N_OFF, SO)
    arrived = jnp.transpose(off_part, (0, 4, 2, 3, 1, 5)).reshape(N_FAULT, N_OFF, quant, face_modes, N_OFF * SO)
    ghosts = jnp.concatenate([lower, upper, arrived], axis=-1)
    return ghosts.reshape(blocks, quant, face_modes, SLOTS)


def reference(modal_state, star_mats, flux_local, flux_nbr, stiff_time, stiff_vol, flux_minus, face_proj, face_turn, face_lift, cluster, send_elem, send_face, nbr_index, orientation, source_elem, source_term):
    blocks = E_TOTAL // E_DEV

    def to_blocks(array):
        shaped = array.reshape(array.shape[:-1] + (blocks, E_DEV))
        return jnp.moveaxis(shaped, -2, 0)

    state_b = to_blocks(modal_state)
    star_b = to_blocks(star_mats)
    local_b = to_blocks(flux_local)
    nbr_b = to_blocks(flux_nbr)
    cluster_b = to_blocks(cluster)
    index_b = to_blocks(nbr_index)
    orient_b = to_blocks(orientation)
    elems_b = send_elem.reshape(blocks, SLOTS)
    faces_b = send_face.reshape(blocks, SLOTS)
    early = weights_over(0.0, HALF_STEP)
    late = weights_over(HALF_STEP, 1.0)

    def phase_one(inputs):
        state_in, star_in, elems_in, faces_in = inputs
        series = predict(state_in, star_in, stiff_time)
        first_half = integrate(series, early)
        second_half = integrate(series, late)
        table_in = traces(first_half, face_proj)
        return first_half, second_half, table_in, jnp.take(table_in, faces_in * E_DEV + elems_in, axis=2)

    first_b, second_b, table_one, sent_one = lax.map(phase_one, (state_b, star_b, elems_b, faces_b))
    ghosts_one = receive(sent_one)

    def phase_two(inputs):
        (state_in, star_in, local_in, nbr_in, cluster_in, index_in, orient_in, first_half, second_half, table_in, ghosts_in, elems_in, faces_in) = inputs
        combined = jnp.concatenate([table_in, ghosts_in], axis=2)
        near_first = jnp.take(combined, index_in, axis=2)
        is_fine = (cluster_in == 1)[None, None, :]
        stepped = update(state_in, first_half, near_first, star_in, local_in, nbr_in, stiff_vol, flux_minus, face_turn, face_lift, orient_in)
        half_state = jnp.where(is_fine, stepped, state_in)
        second_fine = integrate(predict(half_state, star_in, stiff_time), early)
        later_part = jnp.where(is_fine, second_fine, second_half)
        table_out = traces(later_part, face_proj)
        return half_state, later_part, near_first, table_out, jnp.take(table_out, faces_in * E_DEV + elems_in, axis=2)

    half_b, later_b, near_b, table_two, sent_two = lax.map(phase_two, (state_b, star_b, local_b, nbr_b, cluster_b, index_b, orient_b, first_b, second_b, table_one, ghosts_one, elems_b, faces_b))
    ghosts_two = receive(sent_two)

    def phase_three(inputs):
        (state_in, star_in, local_in, nbr_in, cluster_in, index_in, orient_in, first_half, second_half, half_state, later_part, near_first, table_in, ghosts_in) = inputs
        combined = jnp.concatenate([table_in, ghosts_in], axis=2)
        near_second = jnp.take(combined, index_in, axis=2)
        is_fine = (cluster_in == 1)[None, None, :]
        neighbours = jnp.where(is_fine, near_second, near_first + near_second)
        base_state = jnp.where(is_fine, half_state, state_in)
        integral = jnp.where(is_fine, later_part, first_half + second_half)
        return update(base_state, integral, neighbours, star_in, local_in, nbr_in, stiff_vol, flux_minus, face_turn, face_lift, orient_in)

    final_b = lax.map(phase_three, (state_b, star_b, local_b, nbr_b, cluster_b, index_b, orient_b, first_b, second_b, half_b, later_b, near_b, table_two, ghosts_two))
    stepped_all = jnp.moveaxis(final_b, 0, -2).reshape(final_b.shape[1], final_b.shape[2], E_TOTAL)
    return stepped_all.at[:, :, source_elem].add(jnp.transpose(source_term, (1, 2, 0)))
```

```python
import functools
import math

import jax
import jax.numpy as jnp
import numpy as np
from jax import lax
from jax.experimental import pallas as pl
from jax.experimental.pallas import tpu as pltpu
from jax.sharding import PartitionSpec as P

TERMS = 6
HALF_STEP = 0.5
F32 = jnp.float32
BF16 = jnp.bfloat16
MESH = pl.DeviceIdType.MESH
Q = 9
M = 56
J = 21
E = 32
FINE = 16


def weights_over(start, finish):
    return [
        (finish ** (k + 1) - start ** (k + 1)) / math.factorial(k + 1) for k in range(TERMS)
    ]


def split2(x):
    hi = x.astype(BF16)
    return hi, (x - hi.astype(F32)).astype(BF16)


def split3(x):
    hi = x.astype(BF16)
    rest = x - hi.astype(F32)
    mid = rest.astype(BF16)
    return hi, mid, (rest - mid.astype(F32)).astype(BF16)


def dot(a, b):
    return jnp.dot(a, b, preferred_element_type=F32)


def dot_nt(a, b):
    return lax.dot_general(a, b, (((1,), (1,)), ((), ())), preferred_element_type=F32)


def iota(shape, axis):
    return lax.broadcasted_iota(jnp.int32, shape, axis)


def flag(mask):
    return jnp.where(mask, 1.0, 0.0).astype(F32)


def spread_tables():
    lane = np.arange(256)
    star = np.stack([(lane // 64 == 0), (lane // 64 == 1), (lane // 64 >= 2), lane < 0])
    own = np.stack([lane // 64 == f for f in range(4)])
    nbr = np.stack([lane[:128] // 32 == f for f in range(4)])

    def table(pattern):
        width = pattern.shape[1]
        out = np.zeros((4, 2, 4, 4, 8, width), np.float32)
        for i in range(4):
            out[i, :, :, i, :4, :] = pattern
        return out.reshape(4, 256, width)

    return [jnp.asarray(table(t), BF16) for t in (star, own, nbr)]


def kernel(
    n_fault,
    n_off,
    modal_h,
    star_h,
    own_h,
    nbr_h,
    st_h,
    sv_h,
    fm_h,
    proj_h,
    turn_h,
    lift_h,
    cluster_h,
    send_elem_h,
    send_face_h,
    index_h,
    orient_h,
    src_elem_h,
    src_term_h,
    bh_star_h,
    bh_own_h,
    bh_nbr_h,
    out_ref,
    modal,
    star8,
    own8,
    nbr8,
    st,
    sv,
    fm,
    proj,
    turn,
    lift,
    cluster,
    send_elem,
    send_face,
    index,
    orient,
    src_elem,
    src_term,
    bh_star,
    bh_own,
    bh_nbr,
    cs,
    cs2,
    co,
    cn,
    spread_lhs,
    wt32,
    wt,
    wu32,
    wu,
    pw32,
    pw_hi,
    pw_lo,
    state0,
    term,
    first,
    second,
    half,
    later,
    part,
    near1,
    gather_loc,
    gather_rem,
    gather_out,
    rhs,
    send1,
    send2,
    recv1,
    recv2,
    in_sems,
    send_sems,
    recv_sems,
):
    fault = lax.axis_index("fault")
    off = lax.axis_index("off")
    below = lax.rem(fault + n_fault - 1, n_fault)
    above = lax.rem(fault + 1, n_fault)

    star8[...] = jnp.zeros_like(star8)
    own8[...] = jnp.zeros_like(own8)
    nbr8[...] = jnp.zeros_like(nbr8)
    pairs = [
        (cluster_h, cluster),
        (star_h, star8.at[0:81, 0:3, :]),
        (bh_star_h, bh_star),
        (modal_h, modal),
        (st_h, st),
        (index_h, index),
        (send_elem_h, send_elem),
        (send_face_h, send_face),
        (proj_h, proj),
        (own_h, own8.at[0:81, 0:4, :]),
        (bh_own_h, bh_own),
        (sv_h, sv),
        (fm_h, fm),
        (nbr_h, nbr8.at[0:81, 0:4, :]),
        (bh_nbr_h, bh_nbr),
        (orient_h, orient),
        (turn_h, turn),
        (lift_h, lift),
        (src_elem_h, src_elem),
        (src_term_h, src_term),
    ]
    copies = []
    for i, (src, dst) in enumerate(pairs):
        copies.append(pltpu.make_async_copy(src, dst, in_sems.at[i]))
        copies[-1].start()

    barrier = pltpu.get_barrier_semaphore()
    for device in [{"fault": below}, {"fault": above}]:
        pl.semaphore_signal(barrier, inc=1, device_id=device, device_id_type=MESH)
    for step in range(1, n_off):
        pl.semaphore_signal(
            barrier,
            inc=1,
            device_id={"off": lax.rem(off + step, n_off)},
            device_id_type=MESH,
        )

    low_half = iota((16, 128), 1) < 64

    wt32[...] = jnp.zeros_like(wt32)
    wu32[...] = jnp.zeros_like(wu32)
    pw32[...] = jnp.zeros_like(pw32)

    def wait(*which):
        for i in which:
            copies[i].wait()

    wait(0)
    row32 = iota((32, 128), 0)
    lane32 = iota((32, 128), 1)
    col = lane32 & 31
    fine_row = jnp.broadcast_to(cluster[...].astype(F32), (16, 32)).astype(BF16)
    cum = dot(fine_row, flag(row32 <= col).astype(BF16))
    fine4 = dot(fine_row, flag(row32 == col).astype(BF16))
    n_fine = dot(fine_row, jnp.ones((32, 128), BF16))
    col16 = iota((16, 128), 1) & 31
    pos = jnp.where(fine4 > 0.5, cum - 1.0, n_fine + col16.astype(F32) - cum)
    pos = pos.astype(jnp.int32)[0:1]
    is_fine = iota((16, 128), 0).astype(F32) < n_fine
    perm = flag(iota((32, 32), 0) == pos[:, 0:32]).astype(BF16)
    row128 = iota((128, 128), 0)
    lane128 = iota((128, 128), 1)
    perm_big = flag(((row128 >> 5) == (lane128 >> 5)) & ((row128 & 31) == pos)).astype(BF16)

    def spread(rows, table, out, width):
        flat = rows[...].reshape(84 * 8, 32)
        hi, lo = split2(flat)
        g_hi = dot_nt(perm, hi).astype(BF16)
        g_lo = dot_nt(perm, lo).astype(BF16)
        lane = iota((32, 128), 1)
        for tile in range(6):
            hi_t = g_hi[:, 128 * tile : 128 * tile + 128] if tile < 5 else None
            lo_t = g_lo[:, 128 * tile : 128 * tile + 128] if tile < 5 else None
            if tile == 5:
                pad = jnp.zeros((32, 96), BF16)
                hi_t = jnp.concatenate([g_hi[:, 640:672], pad], axis=1)
                lo_t = jnp.concatenate([g_lo[:, 640:672], pad], axis=1)
            for c in range(4 if tile < 5 else 1):
                keep = flag((lane >> 5) == c).astype(BF16)
                chunk = 4 * tile + c
                spread_lhs[32 * chunk : 32 * chunk + 32, 0:128] = hi_t * keep
                spread_lhs[32 * chunk : 32 * chunk + 32, 128:256] = lo_t * keep

        def step(i, carry):
            out[i] = dot(spread_lhs[...], table[i]).reshape(21, 32, width)
            return carry

        lax.fori_loop(0, 4, step, 0)

    wait(1, 2)
    spread(star8, bh_star, cs, 256)

    def coef(table, q, p, rows, lanes):
        qp = Q * q + p
        return table[qp % 4, qp // 4, rows, lanes]

    low32 = iota((32, 128), 1) < 64
    upper = slice(128, 256)
    lower = slice(0, 128)
    whole = slice(0, 32)
    for q in range(Q):
        for pair in range(5):
            a = coef(cs, q, 2 * pair, whole, upper)
            b = coef(cs, q, 2 * pair + 1, whole, upper) if pair < 4 else 0.0
            cs2[q, pair] = jnp.where(low32, a, b)

    wait(4)
    for d in range(4):
        w = st[min(d, 2)]
        wt32[64 * d : 64 * d + M, 0:M] = w
        wt32[64 * d : 64 * d + M, 64 : 64 + M] = w
    w_hi, w_lo = split2(wt32[...])
    wt[:, 0:128] = w_hi
    wt[:, 128:256] = w_lo

    wait(3)
    term[...] = jnp.zeros_like(term)
    for q in range(Q):
        term[q, :, 0:M] = modal[q]
        term[q, :, 64 : 64 + M] = modal[q]
    perm3 = jnp.concatenate([perm, perm, perm], axis=1)
    early = weights_over(0.0, HALF_STEP)
    late = weights_over(HALF_STEP, 1.0)
    for q in range(Q):
        moved = dot(perm3, jnp.concatenate(split3(term[q]), axis=0))
        state0[q] = moved
        term[q] = moved
        first[q] = early[0] * moved
        second[q] = late[0] * moved

    def paired(xs):
        return [jnp.where(low_half, xs[2 * i], xs[2 * i + 1]) for i in range(4)] + [xs[8]]

    def mix_star(xs, xp, q, rows):
        y01 = coef(cs, q, 0, rows, lower) * xs[0]
        for p in range(1, Q):
            y01 = y01 + coef(cs, q, p, rows, lower) * xs[p]
        y2 = cs2[q, 0, rows, :] * xp[0]
        for i in range(1, 5):
            y2 = y2 + cs2[q, i, rows, :] * xp[i]
        return y01, y2

    def product(blocks, weights):
        his, los = [], []
        for row in blocks:
            cut = [split2(b) for b in row]
            his.append(jnp.concatenate([c[0] for c in cut], axis=1))
            los.append(jnp.concatenate([c[1] for c in cut], axis=1))
        both = dot(jnp.concatenate(his, axis=0), weights)
        extra = dot(jnp.concatenate(los, axis=0), weights[:, 0:128])
        return both[:, 0:128] + both[:, 128:256] + extra

    def series_weight(k, values):
        w = jnp.float32(values[TERMS - 1])
        for i in range(1, TERMS - 1):
            w = jnp.where(k == i, jnp.float32(values[i]), w)
        return w

    def predict(halves, sums):
        def step(k, carry):
            for h in range(halves):
                rows = slice(16 * h, 16 * h + 16)
                xs = [term[p, rows, :] for p in range(Q)]
                xp = paired(xs)
                blocks = [list(mix_star(xs, xp, q, rows)) for q in range(Q)]
                made = product(blocks, wt[...])
                for q in range(Q):
                    x = made[16 * q : 16 * q + 16]
                    term[q, rows, :] = x
                    for ref, values in sums:
                        ref[q, rows, :] = ref[q, rows, :] + series_weight(k, values) * x
            return carry

        lax.fori_loop(1, TERMS, step, 0)

    predict(2, [(first, early), (second, late)])

    wait(5, 6, 7)
    tab = iota((128, 32), 0)
    slot = tab & 15
    ghost = jnp.where(
        tab < 32,
        128 + tab,
        jnp.where((slot < 10) & (tab < 96), 160 + 10 * ((tab >> 4) - 2) + slot, -1),
    )
    for f in range(4):
        want = index[f : f + 1, :]
        loc = dot_nt(perm, flag(tab == want).astype(BF16)).astype(BF16)
        loc = dot_nt(loc, perm_big).astype(BF16)
        rem = dot_nt(perm, flag(ghost == want).astype(BF16)).astype(BF16)
        rows = slice(32 * f, 32 * f + 32)
        gather_loc[rows, 0:128] = loc
        gather_loc[rows, 128:256] = loc
        gather_rem[rows, 0:128] = rem
        gather_rem[rows, 128:256] = rem
    wanted = send_face[...] * E + send_elem[...]
    out_hot = flag(iota((128, 72), 0) == wanted).astype(BF16)
    r = iota((96, 72), 0)
    s = iota((96, 72), 1)
    k_in = r & 15
    slot_of = jnp.where(r < 32, r, jnp.where(k_in < 10, 32 + 10 * ((r >> 4) - 2) + k_in, -1))
    picked = dot_nt(flag(slot_of == s).astype(BF16), out_hot).astype(BF16)
    picked = dot_nt(picked, perm_big).astype(BF16)
    gather_out[:, 0:128] = picked
    gather_out[:, 128:256] = picked

    wait(8)
    for f in range(4):
        face = proj[:, f, :]
        for g in range(4):
            start = 128 * f + 32 * g
            pw32[start : start + J, 64 * g : 64 * g + M] = face
    p_hi, p_lo = split2(pw32[...])
    pw_hi[...] = p_hi
    pw_lo[...] = p_lo

    def make_table(integral):
        rows = []
        xs = [integral[q] for q in range(Q)]
        for k in range(2):
            a, b, c, d = xs[4 * k : 4 * k + 4]
            rows.append(
                jnp.concatenate([jnp.where(low32, a, b), jnp.where(low32, c, d)], axis=1)
            )
        rows.append(
            jnp.concatenate([jnp.where(low32, xs[8], 0.0), jnp.zeros((32, 128), F32)], axis=1)
        )
        hi, lo = split2(jnp.concatenate(rows, axis=0))
        faced = dot_nt(hi, pw_hi[...]) + dot_nt(hi, pw_lo[...]) + dot_nt(lo, pw_hi[...])
        for k in range(3):
            for f in range(4):
                t_hi, t_lo = split2(faced[32 * k : 32 * k + 32, 128 * f : 128 * f + 128])
                lanes = slice(128 * k, 128 * k + 128)
                rhs[32 * f : 32 * f + 32, lanes] = t_hi
                rhs[128 + 32 * f : 160 + 32 * f, lanes] = t_lo

    def exchange(sent, received, turn_no):
        outgoing = dot(gather_out[...], rhs[...])
        for a in range(6):
            for k in range(3):
                sent[pl.ds(48 * a + k, 16, stride=3), :] = outgoing[
                    16 * a : 16 * a + 16, 128 * k : 128 * k + 128
                ]
        started = []
        for a, device in enumerate([{"fault": below}, {"fault": above}]):
            started.append(
                pltpu.make_async_remote_copy(
                    src_ref=sent.at[pl.ds(48 * a, 48), :],
                    dst_ref=received.at[1 - a],
                    send_sem=send_sems.at[turn_no, a],
                    recv_sem=recv_sems.at[turn_no, 1 - a],
                    device_id=device,
                    device_id_type=MESH,
                )
            )
            started[-1].start()
        for step in range(1, n_off):
            to = lax.rem(off + step, n_off)
            started.append(
                pltpu.make_async_remote_copy(
                    src_ref=sent.at[pl.ds(pl.multiple_of(96 + 48 * to, 8), 32), :],
                    dst_ref=received.at[2 + off, pl.ds(0, 32), :],
                    send_sem=send_sems.at[turn_no, 1 + step],
                    recv_sem=recv_sems.at[turn_no, 1 + step],
                    device_id={"off": to},
                    device_id_type=MESH,
                )
            )
            started[-1].start()
        received[2 + off] = sent[pl.ds(pl.multiple_of(96 + 48 * off, 8), 48), :]
        return started

    def arrived(started, received):
        for copy in started:
            copy.wait()
        few = iota((16, 128), 0) < 10
        for k in range(3):
            lanes = slice(128 * k, 128 * k + 128)
            for a in range(6):
                piece = received[a, pl.ds(k, 16, stride=3), :]
                if a >= 2:
                    piece = jnp.where(few, piece, 0.0)
                hi, lo = split2(piece)
                rhs[16 * a : 16 * a + 16, lanes] = hi
                rhs[128 + 16 * a : 144 + 16 * a, lanes] = lo
            rhs[96:128, lanes] = jnp.zeros((32, 128), BF16)
            rhs[224:256, lanes] = jnp.zeros((32, 128), BF16)
        return dot(gather_rem[...], rhs[...])

    group = iota((16, 128), 1) >> 5

    def faces_of(near, h):
        made = []
        turned = {}
        for k in range(3):
            for f in range(4):
                base = near(f, k)
                turned[f, k, 0] = base
                shifts = range(1, 4) if k < 2 else [f] if f else []
                for shift in shifts:
                    turned[f, k, shift] = pltpu.roll(base, 32 * shift, 1)
        for q in range(Q):
            k, g = q // 4, q % 4
            out = turned[3, k, (3 - g) % 4]
            for f in (2, 1, 0):
                out = jnp.where(group == f, turned[f, k, (f - g) % 4], out)
            made.append(out)
        return made

    def from_neighbours(near, h):
        rows = slice(16 * h, 16 * h + 16)
        faces = faces_of(near, h)
        facing = coef(cn, Q, 0, rows, lower)
        masks = [flag(facing < 0.5), flag((facing > 0.5) & (facing < 1.5)), flag(facing > 1.5)]
        blocks = []
        for q in range(Q):
            acc = coef(cn, q, 0, rows, lower) * faces[0]
            for p in range(1, Q):
                acc = acc + coef(cn, q, p, rows, lower) * faces[p]
            blocks.append([acc * m for m in masks])
        return product(blocks, wu[512:896, :])

    def from_inside(xs, h):
        rows = slice(16 * h, 16 * h + 16)
        xp = paired(xs)
        blocks = []
        for q in range(Q):
            row = list(mix_star(xs, xp, q, rows))
            for lanes in (lower, upper):
                acc = coef(co, q, 0, rows, lanes) * xs[0]
                for p in range(1, Q):
                    acc = acc + coef(co, q, p, rows, lanes) * xs[p]
                row.append(acc)
            blocks.append(row)
        return product(blocks, wu[0:512, :])

    make_table(first)
    pl.semaphore_wait(barrier, 1 + n_off)
    started = exchange(send1, recv1, 0)

    near1[...] = dot(gather_loc[...], rhs[...])
    wait(9, 10)
    spread(own8, bh_own, co, 256)
    wait(13, 14, 15)
    nbr8[81, 0:4, :] = orient[...].astype(F32)
    spread(nbr8, bh_nbr, cn, 128)
    wait(11, 12, 16, 17)
    for d in range(4):
        w = sv[min(d, 2)]
        wu32[64 * d : 64 * d + M, 0:M] = w
        wu32[64 * d : 64 * d + M, 64 : 64 + M] = w
        w = fm[d]
        wu32[256 + 64 * d : 256 + 64 * d + M, 0:M] = w
        wu32[256 + 64 * d : 256 + 64 * d + M, 64 : 64 + M] = w
    for f in range(4):
        face = lift[:, f, :]
        for o in range(3):
            w = lax.dot_general(
                turn[o],
                face,
                (((1,), (0,)), ((), ())),
                precision=lax.Precision.HIGHEST,
                preferred_element_type=F32,
            )
            start = 512 + 128 * o + 32 * f
            wu32[start : start + J, 0:M] = w
            wu32[start : start + J, 64 : 64 + M] = w
    u_hi, u_lo = split2(wu32[...])
    wu[:, 0:128] = u_hi
    wu[:, 128:256] = u_lo

    inside = from_inside([first[q, 0:16, :] for q in range(Q)], 0)
    for q in range(Q):
        half[q] = state0[q, 0:16, :] + inside[16 * q : 16 * q + 16]
    inside = from_inside([first[q, 16:32, :] + second[q, 16:32, :] for q in range(Q)], 1)
    for q in range(Q):
        part[q, 16:32, :] = state0[q, 16:32, :] + inside[16 * q : 16 * q + 16]

    near1[...] = near1[...] + arrived(started, recv1)
    outside = from_neighbours(
        lambda f, k: near1[32 * f : 32 * f + 16, 128 * k : 128 * k + 128], 0
    )
    for q in range(Q):
        x = half[q] + outside[16 * q : 16 * q + 16]
        x = jnp.where(is_fine, x, state0[q, 0:16, :])
        half[q] = x
        term[q, 0:16, :] = x
        later[q, 0:16, :] = early[0] * x
        later[q, 16:32, :] = second[q, 16:32, :]
    predict(1, [(later, early)])
    for q in range(Q):
        later[q, 0:16, :] = jnp.where(is_fine, later[q, 0:16, :], second[q, 0:16, :])

    make_table(later)
    started = exchange(send2, recv2, 1)

    for f in range(4):
        top = slice(32 * f, 32 * f + 16)
        for k in range(3):
            lanes = slice(128 * k, 128 * k + 128)
            near1[top, lanes] = jnp.where(is_fine, 0.0, near1[top, lanes])
    near1[...] = near1[...] + dot(gather_loc[...], rhs[...])
    inside = from_inside(
        [
            jnp.where(is_fine, later[q, 0:16, :], first[q, 0:16, :] + second[q, 0:16, :])
            for q in range(Q)
        ],
        0,
    )
    for q in range(Q):
        part[q, 0:16, :] = half[q] + inside[16 * q : 16 * q + 16]
    wait(18, 19)
    unperm = dot_nt(flag(iota((32, 32), 0) == iota((32, 32), 1)).astype(BF16), perm).astype(BF16)
    unperm3 = jnp.concatenate([unperm, unperm, unperm], axis=1)
    offset = (fault * n_off + off) * E
    source_hot = flag(iota((32, 16), 0) + offset == src_elem[...]).astype(BF16)
    source_hot3 = jnp.concatenate([source_hot] * 3, axis=1)

    near1[...] = near1[...] + arrived(started, recv2)
    for h in range(2):
        outside = from_neighbours(
            lambda f, k: near1[
                32 * f + 16 * h : 32 * f + 16 * h + 16, 128 * k : 128 * k + 128
            ],
            h,
        )
        for q in range(Q):
            rows = slice(16 * h, 16 * h + 16)
            part[q, rows, :] = part[q, rows, :] + outside[16 * q : 16 * q + 16]
    for q in range(Q):
        made = dot(unperm3, jnp.concatenate(split3(part[q]), axis=0))
        added = dot(source_hot3, jnp.concatenate(split3(src_term[q]), axis=0))
        out_ref[q] = made[:, 0:M] + added


def on_device(
    modal_state,
    star_mats,
    flux_local,
    flux_nbr,
    stiff_time,
    stiff_vol,
    flux_minus,
    face_proj,
    face_turn,
    face_lift,
    cluster,
    send_elem,
    send_face,
    nbr_index,
    orientation,
    source_elem,
    source_term,
):
    n_fault = lax.axis_size("fault")
    n_off = lax.axis_size("off")
    inputs = [
        jnp.transpose(modal_state, (0, 2, 1)),
        jnp.transpose(star_mats, (1, 2, 0, 3)).reshape(81, 3, E),
        jnp.transpose(flux_local, (1, 2, 0, 3)).reshape(81, 4, E),
        jnp.transpose(flux_nbr, (1, 2, 0, 3)).reshape(81, 4, E),
        stiff_time,
        stiff_vol,
        flux_minus,
        jnp.transpose(face_proj, (2, 0, 1)),
        face_turn,
        jnp.transpose(face_lift, (1, 0, 2)),
        cluster.reshape(1, E),
        send_elem.reshape(1, 72),
        send_face.reshape(1, 72),
        nbr_index,
        orientation,
        source_elem.reshape(1, 16),
        jnp.transpose(source_term, (1, 0, 2)),
        *spread_tables(),
    ]
    own = {1: (84, 8, E), 2: (84, 8, E), 3: (84, 8, E)}
    held = [pltpu.VMEM(own.get(i, x.shape), x.dtype) for i, x in enumerate(inputs)]
    scratch = [
        *held,
        pltpu.VMEM((4, 21, E, 256), F32),
        pltpu.VMEM((Q, 5, E, 128), F32),
        pltpu.VMEM((4, 21, E, 256), F32),
        pltpu.VMEM((4, 21, E, 128), F32),
        pltpu.VMEM((21 * E, 256), BF16),
        pltpu.VMEM((256, 128), F32),
        pltpu.VMEM((256, 256), BF16),
        pltpu.VMEM((896, 128), F32),
        pltpu.VMEM((896, 256), BF16),
        pltpu.VMEM((512, 256), F32),
        pltpu.VMEM((512, 256), BF16),
        pltpu.VMEM((512, 256), BF16),
        pltpu.VMEM((Q, E, 128), F32),
        pltpu.VMEM((Q, E, 128), F32),
        pltpu.VMEM((Q, E, 128), F32),
        pltpu.VMEM((Q, E, 128), F32),
        pltpu.VMEM((Q, FINE, 128), F32),
        pltpu.VMEM((Q, E, 128), F32),
        pltpu.VMEM((Q, E, 128), F32),
        pltpu.VMEM((128, 384), F32),
        pltpu.VMEM((128, 256), BF16),
        pltpu.VMEM((128, 256), BF16),
        pltpu.VMEM((96, 256), BF16),
        pltpu.VMEM((256, 384), BF16),
        pltpu.VMEM((288, 128), F32),
        pltpu.VMEM((288, 128), F32),
        pltpu.VMEM((6, 48, 128), F32),
        pltpu.VMEM((6, 48, 128), F32),
        pltpu.SemaphoreType.DMA((len(inputs),)),
        pltpu.SemaphoreType.DMA((2, 5)),
        pltpu.SemaphoreType.DMA((2, 5)),
    ]
    made = pl.pallas_call(
        functools.partial(kernel, n_fault, n_off),
        out_shape=jax.ShapeDtypeStruct((Q, E, M), F32),
        in_specs=[pl.BlockSpec(memory_space=pl.ANY)] * len(inputs),
        out_specs=pl.BlockSpec(memory_space=pltpu.VMEM),
        scratch_shapes=scratch,
        compiler_params=pltpu.CompilerParams(
            collective_id=0, has_side_effects=True, vmem_limit_bytes=56 << 20
        ),
    )(*inputs)
    return jnp.transpose(made, (0, 2, 1))


def solution(mesh):
    in_specs = (
        P(None, None, ("fault", "off")),
        P(None, None, None, ("fault", "off")),
        P(None, None, None, ("fault", "off")),
        P(None, None, None, ("fault", "off")),
        P(),
        P(),
        P(),
        P(),
        P(),
        P(),
        P(("fault", "off")),
        P("fault", "off", None),
        P("fault", "off", None),
        P(None, ("fault", "off")),
        P(None, ("fault", "off")),
        P(),
        P(),
    )
    out_specs = P(None, None, ("fault", "off"))
    return jax.shard_map(
        on_device, mesh=mesh, in_specs=in_specs, out_specs=out_specs, check_vma=False
    )
```

```python
import functools
import math

import jax
import jax.numpy as jnp
import numpy as np
from jax import lax
from jax.experimental import pallas as pl
from jax.experimental.pallas import tpu as pltpu
from jax.sharding import PartitionSpec as P

TERMS = 6
HALF_STEP = 0.5
F32 = jnp.float32
BF16 = jnp.bfloat16
MESH = pl.DeviceIdType.MESH
Q = 9
M = 56
J = 21
E = 32
FINE = 16


def weights_over(start, finish):
    return [
        (finish ** (k + 1) - start ** (k + 1)) / math.factorial(k + 1) for k in range(TERMS)
    ]


def split2(x):
    hi = x.astype(BF16)
    return hi, (x - hi.astype(F32)).astype(BF16)


def split3(x):
    hi = x.astype(BF16)
    rest = x - hi.astype(F32)
    mid = rest.astype(BF16)
    return hi, mid, (rest - mid.astype(F32)).astype(BF16)


def dot(a, b):
    return jnp.dot(a, b, preferred_element_type=F32)


def dot_nt(a, b):
    return lax.dot_general(a, b, (((1,), (1,)), ((), ())), preferred_element_type=F32)


def iota(shape, axis):
    return lax.broadcasted_iota(jnp.int32, shape, axis)


def flag(mask):
    return jnp.where(mask, 1.0, 0.0).astype(F32)


def spread_tables():
    lane = np.arange(256)
    star = np.stack([(lane // 64 == 0), (lane // 64 == 1), (lane // 64 >= 2), lane < 0])
    own = np.stack([lane // 64 == f for f in range(4)])
    nbr = np.stack([lane[:128] // 32 == f for f in range(4)])

    def table(pattern):
        width = pattern.shape[1]
        out = np.zeros((2, 4, 4, 8, 4, width), np.float32)
        for i in range(4):
            out[:, :, i, :4, i, :] = pattern
        out = out.reshape(256, 2, 2 * width)
        return np.ascontiguousarray(out.transpose(1, 0, 2))

    return [jnp.asarray(table(t), BF16) for t in (star, own, nbr)]


def kernel(
    n_fault,
    n_off,
    modal_h,
    star_h,
    own_h,
    nbr_h,
    st_h,
    sv_h,
    fm_h,
    proj_h,
    turn_h,
    lift_h,
    cluster_h,
    send_elem_h,
    send_face_h,
    index_h,
    orient_h,
    src_elem_h,
    bh_star_h,
    bh_own_h,
    bh_nbr_h,
    part,
    hot_ref,
    modal,
    star8,
    own8,
    nbr8,
    st,
    sv,
    fm,
    proj,
    turn,
    lift,
    cluster,
    send_elem,
    send_face,
    index,
    orient,
    src_elem,
    bh_star,
    bh_own,
    bh_nbr,
    cs,
    cs2,
    co,
    cn,
    spread_lhs,
    wt32,
    wt,
    mixed_hi,
    mixed_lo,
    wu32,
    wu,
    pw32,
    pw_hi,
    pw_lo,
    state0,
    term,
    first,
    second,
    half,
    later,
    near1,
    gather_loc,
    gather_rem,
    gather_out,
    rhs,
    send1,
    send2,
    recv1,
    recv2,
    in_sems,
    send_sems,
    recv_sems,
):
    fault = lax.axis_index("fault")
    off = lax.axis_index("off")
    below = lax.rem(fault + n_fault - 1, n_fault)
    above = lax.rem(fault + 1, n_fault)

    star8[...] = jnp.zeros_like(star8)
    own8[...] = jnp.zeros_like(own8)
    nbr8[...] = jnp.zeros_like(nbr8)
    pairs = [
        (cluster_h, cluster),
        (star_h, star8.at[0:81, 0:3, :]),
        (bh_star_h, bh_star),
        (modal_h, modal),
        (st_h, st),
        (index_h, index),
        (send_elem_h, send_elem),
        (send_face_h, send_face),
        (proj_h, proj),
        (own_h, own8.at[0:81, 0:4, :]),
        (bh_own_h, bh_own),
        (sv_h, sv),
        (fm_h, fm),
        (nbr_h, nbr8.at[0:81, 0:4, :]),
        (bh_nbr_h, bh_nbr),
        (orient_h, orient),
        (turn_h, turn),
        (lift_h, lift),
        (src_elem_h, src_elem),
    ]
    copies = []
    for i, (src, dst) in enumerate(pairs):
        copies.append(pltpu.make_async_copy(src, dst, in_sems.at[i]))
        copies[-1].start()

    barrier = pltpu.get_barrier_semaphore()
    for device in [{"fault": below}, {"fault": above}]:
        pl.semaphore_signal(barrier, inc=1, device_id=device, device_id_type=MESH)
    for step in range(1, n_off):
        pl.semaphore_signal(
            barrier,
            inc=1,
            device_id={"off": lax.rem(off + step, n_off)},
            device_id_type=MESH,
        )


    wt32[...] = jnp.zeros_like(wt32)
    wu32[...] = jnp.zeros_like(wu32)
    pw32[...] = jnp.zeros_like(pw32)

    def wait(*which):
        for i in which:
            copies[i].wait()

    wait(0)
    row32 = iota((32, 128), 0)
    lane32 = iota((32, 128), 1)
    col = lane32 & 31
    fine_row = jnp.broadcast_to(cluster[...].astype(F32), (16, 32)).astype(BF16)
    cum = dot(fine_row, flag(row32 <= col).astype(BF16))
    fine4 = dot(fine_row, flag(row32 == col).astype(BF16))
    n_fine = dot(fine_row, jnp.ones((32, 128), BF16))
    col16 = iota((16, 128), 1) & 31
    pos = jnp.where(fine4 > 0.5, cum - 1.0, n_fine + col16.astype(F32) - cum)
    pos = pos.astype(jnp.int32)[0:1]
    is_fine = iota((16, 128), 0).astype(F32) < n_fine
    perm = flag(iota((32, 32), 0) == pos[:, 0:32]).astype(BF16)
    row128 = iota((128, 128), 0)
    lane128 = iota((128, 128), 1)
    perm_big = flag(((row128 >> 5) == (lane128 >> 5)) & ((row128 & 31) == pos)).astype(BF16)

    wait(6, 7)
    wanted = send_face[...] * E + send_elem[...]
    out_hot = flag(iota((128, 72), 0) == wanted).astype(BF16)
    r = iota((96, 72), 0)
    s = iota((96, 72), 1)
    k_in = r & 15
    slot_of = jnp.where(r < 32, r, jnp.where(k_in < 10, 32 + 10 * ((r >> 4) - 2) + k_in, -1))
    picked = dot_nt(flag(slot_of == s).astype(BF16), out_hot).astype(BF16)
    picked = dot_nt(picked, perm_big).astype(BF16)
    gather_out[:, 0:128] = picked
    gather_out[:, 128:256] = picked

    wait(4)
    for d in range(4):
        w = st[min(d, 2)]
        wt32[64 * d : 64 * d + M, 0:M] = w
        wt32[64 * d : 64 * d + M, 64 : 64 + M] = w
    w_hi, w_lo = split2(wt32[...])
    wt[:, 0:128] = w_hi
    wt[:, 128:256] = w_lo

    wait(8)
    for f in range(4):
        face = proj[:, f, :]
        for g in range(4):
            start = 128 * f + 32 * g
            pw32[start : start + J, 64 * g : 64 * g + M] = face
    p_hi, p_lo = split2(pw32[...])
    pw_hi[...] = p_hi
    pw_lo[...] = p_lo

    def spread(rows, table, out, width):
        flat = jnp.transpose(rows[...].reshape(84 * 8, 32))
        hi, lo = split2(flat)
        g_hi = dot(perm, hi).astype(BF16)
        g_lo = dot(perm, lo).astype(BF16)
        lane = iota((32, 128), 1)
        for tile in range(6):
            hi_t = g_hi[:, 128 * tile : 128 * tile + 128] if tile < 5 else None
            lo_t = g_lo[:, 128 * tile : 128 * tile + 128] if tile < 5 else None
            if tile == 5:
                pad = jnp.zeros((32, 96), BF16)
                hi_t = jnp.concatenate([g_hi[:, 640:672], pad], axis=1)
                lo_t = jnp.concatenate([g_lo[:, 640:672], pad], axis=1)
            for c in range(4 if tile < 5 else 1):
                keep = flag((lane >> 5) == c).astype(BF16)
                chunk = 4 * tile + c
                spread_lhs[32 * chunk : 32 * chunk + 32, 0:128] = hi_t * keep
                spread_lhs[32 * chunk : 32 * chunk + 32, 128:256] = lo_t * keep

        def step(i, carry):
            made = dot(spread_lhs[...], table[i])
            out[2 * i] = made[:, 0:width].reshape(21, 32, width)
            out[2 * i + 1] = made[:, width : 2 * width].reshape(21, 32, width)
            return carry

        lax.fori_loop(0, 2, step, 0)

    wait(1, 2)
    spread(star8, bh_star, cs, 256)

    def coef(table, q, p, rows, lanes):
        qp = Q * q + p
        return table[qp % 4, qp // 4, rows, lanes]

    low32 = iota((32, 128), 1) < 64
    upper = slice(128, 256)
    lower = slice(0, 128)
    whole = slice(0, 32)
    for q in range(Q):
        for pair in range(5):
            a = coef(cs, q, 2 * pair, whole, upper)
            b = coef(cs, q, 2 * pair + 1, whole, upper) if pair < 4 else 0.0
            cs2[q, pair] = jnp.where(low32, a, b)

    wait(3)
    term[...] = jnp.zeros_like(term)
    for q in range(Q):
        term[q, :, 0:M] = modal[q]
        term[q, :, 64 : 64 + M] = modal[q]
    perm3 = jnp.concatenate([perm, perm, perm], axis=1)
    early = weights_over(0.0, HALF_STEP)
    late = weights_over(HALF_STEP, 1.0)
    for q in range(Q):
        moved = dot(perm3, jnp.concatenate(split3(term[q]), axis=0))
        state0[q] = moved
        term[q] = moved
        first[q] = early[0] * moved
        second[q] = late[0] * moved

    def paired(xs):
        return [jnp.where(iota(xs[0].shape, 1) < 64, xs[2 * i], xs[2 * i + 1]) for i in range(4)] + [xs[8]]

    def mix_star(xs, xp, q, rows):
        y01 = coef(cs, q, 0, rows, lower) * xs[0]
        for p in range(1, Q):
            y01 = y01 + coef(cs, q, p, rows, lower) * xs[p]
        y2 = cs2[q, 0, rows, :] * xp[0]
        for i in range(1, 5):
            y2 = y2 + cs2[q, i, rows, :] * xp[i]
        return y01, y2

    def cut(blocks):
        his, los = [], []
        for i in range(len(blocks[0])):
            column = [row[i] for row in blocks]
            if column[0].shape[0] % 16:
                column.append(jnp.zeros_like(column[0]))
            hi, lo = split2(jnp.concatenate(column, axis=0))
            his.append(hi)
            los.append(lo)
        return jnp.concatenate(his, axis=1), jnp.concatenate(los, axis=1)

    def contract(hi, lo, weights):
        both = dot(hi, weights)
        extra = dot(lo, weights[:, 0:128])
        return both[:, 0:128] + both[:, 128:256] + extra

    def product(blocks, weights):
        return contract(*cut(blocks), weights)

    def series_weight(k, values):
        w = jnp.float32(values[TERMS - 1])
        for i in range(1, TERMS - 1):
            w = jnp.where(k == i, jnp.float32(values[i]), w)
        return w

    def predict(size, streams, sums):
        filled = (Q * size + 15) // 16 * 16

        def mix(stream):
            rows = slice(size * stream, size * stream + size)
            xs = [term[p, rows, :] for p in range(Q)]
            xp = paired(xs)
            hi, lo = cut([list(mix_star(xs, xp, q, rows)) for q in range(Q)])
            mixed_hi[stream, 0:filled, :] = hi
            mixed_lo[stream, 0:filled, :] = lo

        def expand(stream, k):
            rows = slice(size * stream, size * stream + size)
            made = contract(mixed_hi[stream, 0:filled, :], mixed_lo[stream, 0:filled, :], wt[...])
            for q in range(Q):
                x = made[size * q : size * q + size]
                term[q, rows, :] = x
                for ref, values in sums:
                    ref[q, rows, :] = ref[q, rows, :] + series_weight(k, values) * x

        def step(k, carry):
            expand(0, k)
            mix(1)
            expand(1, k)
            mix(0)
            return carry

        def lone(k, carry):
            mix(0)
            expand(0, k)
            return carry

        if streams == 1:
            lax.fori_loop(1, TERMS, lone, 0)
            return
        mix(0)
        lax.fori_loop(1, TERMS - 1, step, 0)
        expand(0, TERMS - 1)
        mix(1)
        expand(1, TERMS - 1)

    predict(16, 2, [(first, early), (second, late)])

    def make_table(integral):
        rows = []
        xs = [integral[q] for q in range(Q)]
        for k in range(2):
            a, b, c, d = xs[4 * k : 4 * k + 4]
            rows.append(
                jnp.concatenate([jnp.where(low32, a, b), jnp.where(low32, c, d)], axis=1)
            )
        rows.append(
            jnp.concatenate([jnp.where(low32, xs[8], 0.0), jnp.zeros((32, 128), F32)], axis=1)
        )
        hi, lo = split2(jnp.concatenate(rows, axis=0))
        faced = dot_nt(hi, pw_hi[...]) + dot_nt(hi, pw_lo[...]) + dot_nt(lo, pw_hi[...])
        for k in range(3):
            for f in range(4):
                t_hi, t_lo = split2(faced[32 * k : 32 * k + 32, 128 * f : 128 * f + 128])
                lanes = slice(128 * k, 128 * k + 128)
                rhs[32 * f : 32 * f + 32, lanes] = t_hi
                rhs[128 + 32 * f : 160 + 32 * f, lanes] = t_lo

    def exchange(sent, received, turn_no):
        outgoing = dot(gather_out[...], rhs[...])
        for a in range(6):
            for k in range(3):
                sent[pl.ds(48 * a + k, 16, stride=3), :] = outgoing[
                    16 * a : 16 * a + 16, 128 * k : 128 * k + 128
                ]
        started = []
        for step in (2, 1, 3):
            to = lax.rem(off + step, n_off)
            started.append(
                pltpu.make_async_remote_copy(
                    src_ref=sent.at[pl.ds(pl.multiple_of(96 + 48 * to, 8), 32), :],
                    dst_ref=received.at[2 + off, pl.ds(0, 32), :],
                    send_sem=send_sems.at[turn_no, 1 + step],
                    recv_sem=recv_sems.at[turn_no, 1 + step],
                    device_id={"off": to},
                    device_id_type=MESH,
                )
            )
            started[-1].start()
        for a, device in enumerate([{"fault": below}, {"fault": above}]):
            started.append(
                pltpu.make_async_remote_copy(
                    src_ref=sent.at[pl.ds(48 * a, 48), :],
                    dst_ref=received.at[1 - a],
                    send_sem=send_sems.at[turn_no, a],
                    recv_sem=recv_sems.at[turn_no, 1 - a],
                    device_id=device,
                    device_id_type=MESH,
                )
            )
            started[-1].start()
        received[2 + off] = sent[pl.ds(pl.multiple_of(96 + 48 * off, 8), 48), :]
        return started

    def arrived(started, received):
        for copy in started:
            copy.wait()
        few = iota((16, 128), 0) < 10
        for k in range(3):
            lanes = slice(128 * k, 128 * k + 128)
            for a in range(6):
                piece = received[a, pl.ds(k, 16, stride=3), :]
                if a >= 2:
                    piece = jnp.where(few, piece, 0.0)
                hi, lo = split2(piece)
                rhs[16 * a : 16 * a + 16, lanes] = hi
                rhs[128 + 16 * a : 144 + 16 * a, lanes] = lo
            rhs[96:128, lanes] = jnp.zeros((32, 128), BF16)
            rhs[224:256, lanes] = jnp.zeros((32, 128), BF16)
        return dot(gather_rem[...], rhs[...])

    group = iota((16, 128), 1) >> 5

    def faces_of(near, h):
        made = []
        turned = {}
        for k in range(3):
            for f in range(4):
                base = near(f, k)
                turned[f, k, 0] = base
                shifts = range(1, 4) if k < 2 else [f] if f else []
                for shift in shifts:
                    turned[f, k, shift] = pltpu.roll(base, 32 * shift, 1)
        for q in range(Q):
            k, g = q // 4, q % 4
            out = turned[3, k, (3 - g) % 4]
            for f in (2, 1, 0):
                out = jnp.where(group == f, turned[f, k, (f - g) % 4], out)
            made.append(out)
        return made

    def from_neighbours(near, h):
        rows = slice(16 * h, 16 * h + 16)
        faces = faces_of(near, h)
        facing = coef(cn, Q, 0, rows, lower)
        masks = [flag(facing < 0.5), flag((facing > 0.5) & (facing < 1.5)), flag(facing > 1.5)]
        blocks = []
        for q in range(Q):
            acc = coef(cn, q, 0, rows, lower) * faces[0]
            for p in range(1, Q):
                acc = acc + coef(cn, q, p, rows, lower) * faces[p]
            blocks.append([acc * m for m in masks])
        return product(blocks, wu[512:896, :])

    def from_inside(xs, h):
        rows = slice(16 * h, 16 * h + 16)
        xp = paired(xs)
        blocks = []
        for q in range(Q):
            row = list(mix_star(xs, xp, q, rows))
            for lanes in (lower, upper):
                acc = coef(co, q, 0, rows, lanes) * xs[0]
                for p in range(1, Q):
                    acc = acc + coef(co, q, p, rows, lanes) * xs[p]
                row.append(acc)
            blocks.append(row)
        return product(blocks, wu[0:512, :])

    make_table(first)
    pl.semaphore_wait(barrier, 1 + n_off)
    started = exchange(send1, recv1, 0)

    wait(5)
    tab = iota((128, 32), 0)
    slot = tab & 15
    ghost = jnp.where(
        tab < 32,
        128 + tab,
        jnp.where((slot < 10) & (tab < 96), 160 + 10 * ((tab >> 4) - 2) + slot, -1),
    )
    for f in range(4):
        want = index[f : f + 1, :]
        loc = dot_nt(perm, flag(tab == want).astype(BF16)).astype(BF16)
        loc = dot_nt(loc, perm_big).astype(BF16)
        rem = dot_nt(perm, flag(ghost == want).astype(BF16)).astype(BF16)
        rows = slice(32 * f, 32 * f + 32)
        gather_loc[rows, 0:128] = loc
        gather_loc[rows, 128:256] = loc
        gather_rem[rows, 0:128] = rem
        gather_rem[rows, 128:256] = rem
    near1[...] = dot(gather_loc[...], rhs[...])
    wait(9, 10)
    spread(own8, bh_own, co, 256)
    wait(13, 14, 15)
    nbr8[81, 0:4, :] = orient[...].astype(F32)
    spread(nbr8, bh_nbr, cn, 128)
    wait(11, 12, 16, 17)
    for d in range(4):
        w = sv[min(d, 2)]
        wu32[64 * d : 64 * d + M, 0:M] = w
        wu32[64 * d : 64 * d + M, 64 : 64 + M] = w
        w = fm[d]
        wu32[256 + 64 * d : 256 + 64 * d + M, 0:M] = w
        wu32[256 + 64 * d : 256 + 64 * d + M, 64 : 64 + M] = w
    for f in range(4):
        face = lift[:, f, :]
        for o in range(3):
            w = lax.dot_general(
                turn[o],
                face,
                (((1,), (0,)), ((), ())),
                precision=lax.Precision.HIGHEST,
                preferred_element_type=F32,
            )
            start = 512 + 128 * o + 32 * f
            wu32[start : start + J, 0:M] = w
            wu32[start : start + J, 64 : 64 + M] = w
    u_hi, u_lo = split2(wu32[...])
    wu[:, 0:128] = u_hi
    wu[:, 128:256] = u_lo

    inside = from_inside([first[q, 0:16, :] for q in range(Q)], 0)
    for q in range(Q):
        half[q] = state0[q, 0:16, :] + inside[16 * q : 16 * q + 16]
    inside = from_inside([first[q, 16:32, :] + second[q, 16:32, :] for q in range(Q)], 1)
    for q in range(Q):
        part[q, 16:32, :] = state0[q, 16:32, :] + inside[16 * q : 16 * q + 16]

    near1[...] = near1[...] + arrived(started, recv1)
    outside = from_neighbours(
        lambda f, k: near1[32 * f : 32 * f + 16, 128 * k : 128 * k + 128], 0
    )
    for q in range(Q):
        x = half[q] + outside[16 * q : 16 * q + 16]
        x = jnp.where(is_fine, x, state0[q, 0:16, :])
        half[q] = x
        term[q, 0:16, :] = x
        later[q, 0:16, :] = early[0] * x
        later[q, 16:32, :] = second[q, 16:32, :]
    predict(16, 1, [(later, early)])
    for q in range(Q):
        later[q, 0:16, :] = jnp.where(is_fine, later[q, 0:16, :], second[q, 0:16, :])

    make_table(later)
    started = exchange(send2, recv2, 1)

    for f in range(4):
        top = slice(32 * f, 32 * f + 16)
        for k in range(3):
            lanes = slice(128 * k, 128 * k + 128)
            near1[top, lanes] = jnp.where(is_fine, 0.0, near1[top, lanes])
    near1[...] = near1[...] + dot(gather_loc[...], rhs[...])
    inside = from_inside(
        [
            jnp.where(is_fine, later[q, 0:16, :], first[q, 0:16, :] + second[q, 0:16, :])
            for q in range(Q)
        ],
        0,
    )
    for q in range(Q):
        part[q, 0:16, :] = half[q] + inside[16 * q : 16 * q + 16]
    wait(18)
    unperm = dot_nt(flag(iota((32, 32), 0) == iota((32, 32), 1)).astype(BF16), perm).astype(BF16)
    unperm3 = jnp.concatenate([unperm, unperm, unperm], axis=1)
    offset = (fault * n_off + off) * E
    source_hot = flag(iota((32, 16), 0) + offset == src_elem[...]).astype(BF16)
    source_hot3 = jnp.concatenate([source_hot] * 3, axis=1)

    near1[...] = near1[...] + arrived(started, recv2)
    for h in range(2):
        outside = from_neighbours(
            lambda f, k: near1[
                32 * f + 16 * h : 32 * f + 16 * h + 16, 128 * k : 128 * k + 128
            ],
            h,
        )
        for q in range(Q):
            rows = slice(16 * h, 16 * h + 16)
            part[q, rows, :] = part[q, rows, :] + outside[16 * q : 16 * q + 16]
    hot_ref[:, 0:96] = unperm3
    hot_ref[:, 96:144] = source_hot3


def finish(part, hot, src_term, out_ref):
    for q in range(Q):
        moved = jnp.concatenate(split3(part[q][:, 0:M]), axis=0)
        added = jnp.concatenate(split3(src_term[q]), axis=0)
        out_ref[q] = dot(hot[:, 0:96], moved) + dot(hot[:, 96:144], added)


def on_device(
    modal_state,
    star_mats,
    flux_local,
    flux_nbr,
    stiff_time,
    stiff_vol,
    flux_minus,
    face_proj,
    face_turn,
    face_lift,
    cluster,
    send_elem,
    send_face,
    nbr_index,
    orientation,
    source_elem,
    source_term,
):
    n_fault = lax.axis_size("fault")
    n_off = lax.axis_size("off")
    inputs = [
        jnp.transpose(modal_state, (0, 2, 1)),
        jnp.transpose(star_mats, (1, 2, 0, 3)).reshape(81, 3, E),
        jnp.transpose(flux_local, (1, 2, 0, 3)).reshape(81, 4, E),
        jnp.transpose(flux_nbr, (1, 2, 0, 3)).reshape(81, 4, E),
        stiff_time,
        stiff_vol,
        flux_minus,
        jnp.transpose(face_proj, (2, 0, 1)),
        face_turn,
        jnp.transpose(face_lift, (1, 0, 2)),
        cluster.reshape(1, E),
        send_elem.reshape(1, 72),
        send_face.reshape(1, 72),
        nbr_index,
        orientation,
        source_elem.reshape(1, 16),
        *spread_tables(),
    ]
    own = {1: (84, 8, E), 2: (84, 8, E), 3: (84, 8, E)}
    held = [pltpu.VMEM(own.get(i, x.shape), x.dtype) for i, x in enumerate(inputs)]
    scratch = [
        *held,
        pltpu.VMEM((4, 21, E, 256), F32),
        pltpu.VMEM((Q, 5, E, 128), F32),
        pltpu.VMEM((4, 21, E, 256), F32),
        pltpu.VMEM((4, 21, E, 128), F32),
        pltpu.VMEM((21 * E, 256), BF16),
        pltpu.VMEM((256, 128), F32),
        pltpu.VMEM((256, 256), BF16),
        pltpu.VMEM((2, 144, 256), BF16),
        pltpu.VMEM((2, 144, 256), BF16),
        pltpu.VMEM((896, 128), F32),
        pltpu.VMEM((896, 256), BF16),
        pltpu.VMEM((512, 256), F32),
        pltpu.VMEM((512, 256), BF16),
        pltpu.VMEM((512, 256), BF16),
        pltpu.VMEM((Q, E, 128), F32),
        pltpu.VMEM((Q, E, 128), F32),
        pltpu.VMEM((Q, E, 128), F32),
        pltpu.VMEM((Q, E, 128), F32),
        pltpu.VMEM((Q, FINE, 128), F32),
        pltpu.VMEM((Q, E, 128), F32),
        pltpu.VMEM((128, 384), F32),
        pltpu.VMEM((128, 256), BF16),
        pltpu.VMEM((128, 256), BF16),
        pltpu.VMEM((96, 256), BF16),
        pltpu.VMEM((256, 384), BF16),
        pltpu.VMEM((288, 128), F32),
        pltpu.VMEM((288, 128), F32),
        pltpu.VMEM((6, 48, 128), F32),
        pltpu.VMEM((6, 48, 128), F32),
        pltpu.SemaphoreType.DMA((len(inputs),)),
        pltpu.SemaphoreType.DMA((2, 5)),
        pltpu.SemaphoreType.DMA((2, 5)),
    ]
    part, hot = pl.pallas_call(
        functools.partial(kernel, n_fault, n_off),
        out_shape=[
            jax.ShapeDtypeStruct((Q, E, 128), F32),
            jax.ShapeDtypeStruct((E, 144), BF16),
        ],
        in_specs=[pl.BlockSpec(memory_space=pl.ANY)] * len(inputs),
        out_specs=[pl.BlockSpec(memory_space=pltpu.VMEM)] * 2,
        scratch_shapes=scratch,
        compiler_params=pltpu.CompilerParams(
            collective_id=0, has_side_effects=True, vmem_limit_bytes=56 << 20
        ),
    )(*inputs)
    made = pl.pallas_call(
        finish,
        out_shape=jax.ShapeDtypeStruct((Q, E, M), F32),
        in_specs=[pl.BlockSpec(memory_space=pltpu.VMEM)] * 3,
        out_specs=pl.BlockSpec(memory_space=pltpu.VMEM),
    )(part, hot, jnp.transpose(source_term, (1, 0, 2)))
    return jnp.transpose(made, (0, 2, 1))


def solution(mesh):
    in_specs = (
        P(None, None, ("fault", "off")),
        P(None, None, None, ("fault", "off")),
        P(None, None, None, ("fault", "off")),
        P(None, None, None, ("fault", "off")),
        P(),
        P(),
        P(),
        P(),
        P(),
        P(),
        P(("fault", "off")),
        P("fault", "off", None),
        P("fault", "off", None),
        P(None, ("fault", "off")),
        P(None, ("fault", "off")),
        P(),
        P(),
    )
    out_specs = P(None, None, ("fault", "off"))
    return jax.shard_map(
        on_device, mesh=mesh, in_specs=in_specs, out_specs=out_specs, check_vma=False
    )
```

```python
import functools
import math

import jax
import jax.numpy as jnp
import numpy as np
from jax import lax
from jax.experimental import pallas as pl
from jax.experimental.pallas import tpu as pltpu
from jax.sharding import PartitionSpec as P

TERMS = 6
HALF_STEP = 0.5
F32 = jnp.float32
BF16 = jnp.bfloat16
MESH = pl.DeviceIdType.MESH
Q = 9
M = 56
J = 21
E = 32
FINE = 16


def weights_over(start, finish):
    return [
        (finish ** (k + 1) - start ** (k + 1)) / math.factorial(k + 1) for k in range(TERMS)
    ]


def split2(x):
    hi = x.astype(BF16)
    return hi, (x - hi.astype(F32)).astype(BF16)


def split3(x):
    hi = x.astype(BF16)
    rest = x - hi.astype(F32)
    mid = rest.astype(BF16)
    return hi, mid, (rest - mid.astype(F32)).astype(BF16)


def dot(a, b):
    return jnp.dot(a, b, preferred_element_type=F32)


def dot_nt(a, b):
    return lax.dot_general(a, b, (((1,), (1,)), ((), ())), preferred_element_type=F32)


def iota(shape, axis):
    return lax.broadcasted_iota(jnp.int32, shape, axis)


def flag(mask):
    return jnp.where(mask, 1.0, 0.0).astype(F32)


def spread_tables():
    lane = np.arange(256)
    star = np.stack([(lane // 64 == 0), (lane // 64 == 1), (lane // 64 >= 2), lane < 0])
    own = np.stack([lane // 64 == f for f in range(4)])
    nbr = np.stack([lane[:128] // 32 == f for f in range(4)])

    def table(pattern):
        width = pattern.shape[1]
        out = np.zeros((2, 4, 4, 8, 4, width), np.float32)
        for i in range(4):
            out[:, :, i, :4, i, :] = pattern
        out = out.reshape(256, 2, 2 * width)
        return np.ascontiguousarray(out.transpose(1, 0, 2))

    return [jnp.asarray(table(t), BF16) for t in (star, own, nbr)]


def kernel(
    n_fault,
    n_off,
    modal_h,
    star_h,
    own_h,
    nbr_h,
    st_h,
    sv_h,
    fm_h,
    proj_h,
    turn_h,
    lift_h,
    cluster_h,
    send_elem_h,
    send_face_h,
    index_h,
    orient_h,
    src_elem_h,
    bh_star_h,
    bh_own_h,
    bh_nbr_h,
    part,
    hot_ref,
    modal,
    star8,
    own8,
    nbr8,
    st,
    sv,
    fm,
    proj,
    turn,
    lift,
    cluster,
    send_elem,
    send_face,
    index,
    orient,
    src_elem,
    bh_star,
    bh_own,
    bh_nbr,
    cs,
    cs2,
    co,
    cn,
    spread_lhs,
    wt32,
    wt,
    mixed_hi,
    mixed_lo,
    wu32,
    wu,
    pw32,
    pw_hi,
    pw_lo,
    state0,
    term,
    first,
    second,
    half,
    later,
    near1,
    gather_loc,
    gather_rem,
    gather_out,
    rhs,
    send1,
    send2,
    recv1,
    recv2,
    in_sems,
    send_sems,
    recv_sems,
):
    fault = lax.axis_index("fault")
    off = lax.axis_index("off")
    below = lax.rem(fault + n_fault - 1, n_fault)
    above = lax.rem(fault + 1, n_fault)

    star8[...] = jnp.zeros_like(star8)
    own8[...] = jnp.zeros_like(own8)
    nbr8[...] = jnp.zeros_like(nbr8)
    pairs = [
        (cluster_h, cluster),
        (star_h, star8.at[0:81, 0:3, :]),
        (bh_star_h, bh_star),
        (modal_h, modal),
        (st_h, st),
        (index_h, index),
        (send_elem_h, send_elem),
        (send_face_h, send_face),
        (proj_h, proj),
        (own_h, own8.at[0:81, 0:4, :]),
        (bh_own_h, bh_own),
        (sv_h, sv),
        (fm_h, fm),
        (nbr_h, nbr8.at[0:81, 0:4, :]),
        (bh_nbr_h, bh_nbr),
        (orient_h, orient),
        (turn_h, turn),
        (lift_h, lift),
        (src_elem_h, src_elem),
    ]
    copies = []
    for i, (src, dst) in enumerate(pairs):
        copies.append(pltpu.make_async_copy(src, dst, in_sems.at[i]))
        copies[-1].start()

    barrier = pltpu.get_barrier_semaphore()
    for device in [{"fault": below}, {"fault": above}]:
        pl.semaphore_signal(barrier, inc=1, device_id=device, device_id_type=MESH)
    for step in range(1, n_off):
        pl.semaphore_signal(
            barrier,
            inc=1,
            device_id={"off": lax.rem(off + step, n_off)},
            device_id_type=MESH,
        )


    wt32[...] = jnp.zeros_like(wt32)
    wu32[...] = jnp.zeros_like(wu32)
    pw32[...] = jnp.zeros_like(pw32)

    def wait(*which):
        for i in which:
            copies[i].wait()

    wait(0)
    row32 = iota((32, 128), 0)
    lane32 = iota((32, 128), 1)
    col = lane32 & 31
    fine_row = jnp.broadcast_to(cluster[...].astype(F32), (16, 32)).astype(BF16)
    cum = dot(fine_row, flag(row32 <= col).astype(BF16))
    fine4 = dot(fine_row, flag(row32 == col).astype(BF16))
    n_fine = dot(fine_row, jnp.ones((32, 128), BF16))
    col16 = iota((16, 128), 1) & 31
    pos = jnp.where(fine4 > 0.5, cum - 1.0, n_fine + col16.astype(F32) - cum)
    pos = pos.astype(jnp.int32)[0:1]
    is_fine = iota((16, 128), 0).astype(F32) < n_fine
    perm = flag(iota((32, 32), 0) == pos[:, 0:32]).astype(BF16)
    row128 = iota((128, 128), 0)
    lane128 = iota((128, 128), 1)
    perm_big = flag(((row128 >> 5) == (lane128 >> 5)) & ((row128 & 31) == pos)).astype(BF16)

    wait(6, 7)
    wanted = send_face[...] * E + send_elem[...]
    out_hot = flag(iota((128, 72), 0) == wanted).astype(BF16)
    r = iota((96, 72), 0)
    s = iota((96, 72), 1)
    k_in = r & 15
    slot_of = jnp.where(r < 32, r, jnp.where(k_in < 10, 32 + 10 * ((r >> 4) - 2) + k_in, -1))
    picked = dot_nt(flag(slot_of == s).astype(BF16), out_hot).astype(BF16)
    picked = dot_nt(picked, perm_big).astype(BF16)
    gather_out[:, 0:128] = picked
    gather_out[:, 128:256] = picked

    wait(4)
    for d in range(4):
        w = st[min(d, 2)]
        wt32[64 * d : 64 * d + M, 0:M] = w
        wt32[64 * d : 64 * d + M, 64 : 64 + M] = w
    w_hi, w_lo = split2(wt32[...])
    wt[:, 0:128] = w_hi
    wt[:, 128:256] = w_lo

    wait(8)
    for f in range(4):
        face = proj[:, f, :]
        for g in range(4):
            start = 128 * f + 32 * g
            pw32[start : start + J, 64 * g : 64 * g + M] = face
    p_hi, p_lo = split2(jnp.transpose(pw32[...]))
    pw_hi[...] = p_hi
    pw_lo[...] = p_lo

    def spread(rows, table, out, width):
        flat = jnp.transpose(rows[...].reshape(84 * 8, 32))
        hi, lo = split2(flat)
        g_hi = dot(perm, hi).astype(BF16)
        g_lo = dot(perm, lo).astype(BF16)
        lane = iota((32, 128), 1)
        for tile in range(6):
            hi_t = g_hi[:, 128 * tile : 128 * tile + 128] if tile < 5 else None
            lo_t = g_lo[:, 128 * tile : 128 * tile + 128] if tile < 5 else None
            if tile == 5:
                pad = jnp.zeros((32, 96), BF16)
                hi_t = jnp.concatenate([g_hi[:, 640:672], pad], axis=1)
                lo_t = jnp.concatenate([g_lo[:, 640:672], pad], axis=1)
            for c in range(4 if tile < 5 else 1):
                keep = flag((lane >> 5) == c).astype(BF16)
                chunk = 4 * tile + c
                spread_lhs[32 * chunk : 32 * chunk + 32, 0:128] = hi_t * keep
                spread_lhs[32 * chunk : 32 * chunk + 32, 128:256] = lo_t * keep

        def step(i, carry):
            made = dot(spread_lhs[...], table[i])
            out[2 * i] = made[:, 0:width].reshape(21, 32, width)
            out[2 * i + 1] = made[:, width : 2 * width].reshape(21, 32, width)
            return carry

        step(0, 0)
        step(1, 0)

    wait(1, 2)
    spread(star8, bh_star, cs, 256)

    def coef(table, q, p, rows, lanes):
        qp = Q * q + p
        return table[qp % 4, qp // 4, rows, lanes]

    low32 = iota((32, 128), 1) < 64
    upper = slice(128, 256)
    lower = slice(0, 128)
    whole = slice(0, 32)
    for q in range(Q):
        for pair in range(5):
            a = coef(cs, q, 2 * pair, whole, upper)
            b = coef(cs, q, 2 * pair + 1, whole, upper) if pair < 4 else 0.0
            cs2[q, pair] = jnp.where(low32, a, b)

    wait(3)
    term[...] = jnp.zeros_like(term)
    for q in range(Q):
        term[q, :, 0:M] = modal[q]
        term[q, :, 64 : 64 + M] = modal[q]
    perm3 = jnp.concatenate([perm, perm, perm], axis=1)
    early = weights_over(0.0, HALF_STEP)
    late = weights_over(HALF_STEP, 1.0)
    for q in range(Q):
        moved = dot(perm3, jnp.concatenate(split3(term[q]), axis=0))
        state0[q] = moved
        term[q] = moved
        first[q] = early[0] * moved
        second[q] = late[0] * moved

    def paired(xs):
        return [jnp.where(iota(xs[0].shape, 1) < 64, xs[2 * i], xs[2 * i + 1]) for i in range(4)] + [xs[8]]

    def mix_star(xs, xp, q, rows):
        y01 = coef(cs, q, 0, rows, lower) * xs[0]
        for p in range(1, Q):
            y01 = y01 + coef(cs, q, p, rows, lower) * xs[p]
        y2 = cs2[q, 0, rows, :] * xp[0]
        for i in range(1, 5):
            y2 = y2 + cs2[q, i, rows, :] * xp[i]
        return y01, y2

    def cut(blocks):
        his, los = [], []
        for i in range(len(blocks[0])):
            column = [row[i] for row in blocks]
            if column[0].shape[0] % 16:
                column.append(jnp.zeros_like(column[0]))
            hi, lo = split2(jnp.concatenate(column, axis=0))
            his.append(hi)
            los.append(lo)
        return jnp.concatenate(his, axis=1), jnp.concatenate(los, axis=1)

    def contract(hi, lo, weights):
        both = dot(hi, weights)
        extra = dot(lo, weights[:, 0:128])
        return both[:, 0:128] + both[:, 128:256] + extra

    def product(blocks, weights):
        return contract(*cut(blocks), weights)

    def series_weight(k, values):
        w = jnp.float32(values[TERMS - 1])
        for i in range(1, TERMS - 1):
            w = jnp.where(k == i, jnp.float32(values[i]), w)
        return w

    def predict(size, streams, sums):
        filled = (Q * size + 15) // 16 * 16

        def mix(stream):
            rows = slice(size * stream, size * stream + size)
            xs = [term[p, rows, :] for p in range(Q)]
            xp = paired(xs)
            hi, lo = cut([list(mix_star(xs, xp, q, rows)) for q in range(Q)])
            mixed_hi[stream, 0:filled, :] = hi
            mixed_lo[stream, 0:filled, :] = lo

        def expand(stream, k):
            rows = slice(size * stream, size * stream + size)
            made = contract(mixed_hi[stream, 0:filled, :], mixed_lo[stream, 0:filled, :], wt[...])
            for q in range(Q):
                x = made[size * q : size * q + size]
                term[q, rows, :] = x
                for ref, values in sums:
                    ref[q, rows, :] = ref[q, rows, :] + series_weight(k, values) * x

        def step(k, carry):
            expand(0, k)
            mix(1)
            expand(1, k)
            mix(0)
            return carry

        def lone(k, carry):
            mix(0)
            expand(0, k)
            return carry

        if streams == 1:
            lax.fori_loop(1, TERMS, lone, 0)
            return
        mix(0)
        lax.fori_loop(1, TERMS - 1, step, 0)
        expand(0, TERMS - 1)
        mix(1)
        expand(1, TERMS - 1)

    predict(16, 2, [(first, early), (second, late)])

    def make_table(integral):
        rows = []
        xs = [integral[q] for q in range(Q)]
        for k in range(2):
            a, b, c, d = xs[4 * k : 4 * k + 4]
            rows.append(
                jnp.concatenate([jnp.where(low32, a, b), jnp.where(low32, c, d)], axis=1)
            )
        rows.append(
            jnp.concatenate([jnp.where(low32, xs[8], 0.0), jnp.zeros((32, 128), F32)], axis=1)
        )
        hi, lo = split2(jnp.concatenate(rows, axis=0))
        both = dot(jnp.concatenate([hi, lo], axis=0), pw_hi[...])
        faced = both[0:96] + both[96:192] + dot(hi, pw_lo[...])
        for k in range(3):
            for f in range(4):
                t_hi, t_lo = split2(faced[32 * k : 32 * k + 32, 128 * f : 128 * f + 128])
                lanes = slice(128 * k, 128 * k + 128)
                rhs[32 * f : 32 * f + 32, lanes] = t_hi
                rhs[128 + 32 * f : 160 + 32 * f, lanes] = t_lo

    def exchange(sent, received, turn_no):
        outgoing = dot(gather_out[...], rhs[...])

        def store(slots):
            for a in slots:
                for k in range(3):
                    sent[pl.ds(48 * a + k, 16, stride=3), :] = outgoing[
                        16 * a : 16 * a + 16, 128 * k : 128 * k + 128
                    ]

        store(range(2, 6))
        started = []
        for step in (2, 1, 3):
            to = lax.rem(off + step, n_off)
            started.append(
                pltpu.make_async_remote_copy(
                    src_ref=sent.at[pl.ds(pl.multiple_of(96 + 48 * to, 8), 32), :],
                    dst_ref=received.at[2 + off, pl.ds(0, 32), :],
                    send_sem=send_sems.at[turn_no, 1 + step],
                    recv_sem=recv_sems.at[turn_no, 1 + step],
                    device_id={"off": to},
                    device_id_type=MESH,
                )
            )
            started[-1].start()
        store(range(2))
        for a, device in enumerate([{"fault": below}, {"fault": above}]):
            started.append(
                pltpu.make_async_remote_copy(
                    src_ref=sent.at[pl.ds(48 * a, 48), :],
                    dst_ref=received.at[1 - a],
                    send_sem=send_sems.at[turn_no, a],
                    recv_sem=recv_sems.at[turn_no, 1 - a],
                    device_id=device,
                    device_id_type=MESH,
                )
            )
            started[-1].start()
        received[2 + off] = sent[pl.ds(pl.multiple_of(96 + 48 * off, 8), 48), :]
        return started

    def arrived(started, received):
        for copy in started:
            copy.wait()
        few = iota((16, 128), 0) < 10
        for k in range(3):
            lanes = slice(128 * k, 128 * k + 128)
            for a in range(6):
                piece = received[a, pl.ds(k, 16, stride=3), :]
                if a >= 2:
                    piece = jnp.where(few, piece, 0.0)
                hi, lo = split2(piece)
                rhs[16 * a : 16 * a + 16, lanes] = hi
                rhs[128 + 16 * a : 144 + 16 * a, lanes] = lo
            rhs[96:128, lanes] = jnp.zeros((32, 128), BF16)
            rhs[224:256, lanes] = jnp.zeros((32, 128), BF16)
        return dot(gather_rem[...], rhs[...])

    group = iota((16, 128), 1) >> 5

    def faces_of(near, h):
        made = []
        turned = {}
        for k in range(3):
            for f in range(4):
                base = near(f, k)
                turned[f, k, 0] = base
                shifts = range(1, 4) if k < 2 else [f] if f else []
                for shift in shifts:
                    turned[f, k, shift] = pltpu.roll(base, 32 * shift, 1)
        for q in range(Q):
            k, g = q // 4, q % 4
            out = turned[3, k, (3 - g) % 4]
            for f in (2, 1, 0):
                out = jnp.where(group == f, turned[f, k, (f - g) % 4], out)
            made.append(out)
        return made

    def from_neighbours(near, h):
        rows = slice(16 * h, 16 * h + 16)
        faces = faces_of(near, h)
        facing = coef(cn, Q, 0, rows, lower)
        masks = [flag(facing < 0.5), flag((facing > 0.5) & (facing < 1.5)), flag(facing > 1.5)]
        blocks = []
        for q in range(Q):
            acc = coef(cn, q, 0, rows, lower) * faces[0]
            for p in range(1, Q):
                acc = acc + coef(cn, q, p, rows, lower) * faces[p]
            blocks.append([acc * m for m in masks])
        return product(blocks, wu[512:896, :])

    def from_inside(xs, h):
        rows = slice(16 * h, 16 * h + 16)
        xp = paired(xs)
        blocks = []
        for q in range(Q):
            row = list(mix_star(xs, xp, q, rows))
            for lanes in (lower, upper):
                acc = coef(co, q, 0, rows, lanes) * xs[0]
                for p in range(1, Q):
                    acc = acc + coef(co, q, p, rows, lanes) * xs[p]
                row.append(acc)
            blocks.append(row)
        return product(blocks, wu[0:512, :])

    make_table(first)
    pl.semaphore_wait(barrier, 1 + n_off)
    started = exchange(send1, recv1, 0)

    wait(5)
    tab = iota((128, 32), 0)
    slot = tab & 15
    ghost = jnp.where(
        tab < 32,
        128 + tab,
        jnp.where((slot < 10) & (tab < 96), 160 + 10 * ((tab >> 4) - 2) + slot, -1),
    )
    for f in range(4):
        want = index[f : f + 1, :]
        loc = dot_nt(perm, flag(tab == want).astype(BF16)).astype(BF16)
        loc = dot_nt(loc, perm_big).astype(BF16)
        rem = dot_nt(perm, flag(ghost == want).astype(BF16)).astype(BF16)
        rows = slice(32 * f, 32 * f + 32)
        gather_loc[rows, 0:128] = loc
        gather_loc[rows, 128:256] = loc
        gather_rem[rows, 0:128] = rem
        gather_rem[rows, 128:256] = rem
    near1[...] = dot(gather_loc[...], rhs[...])
    wait(9, 10)
    spread(own8, bh_own, co, 256)
    wait(13, 14, 15)
    nbr8[81, 0:4, :] = orient[...].astype(F32)
    spread(nbr8, bh_nbr, cn, 128)
    wait(11, 12, 16, 17)
    for d in range(4):
        w = sv[min(d, 2)]
        wu32[64 * d : 64 * d + M, 0:M] = w
        wu32[64 * d : 64 * d + M, 64 : 64 + M] = w
        w = fm[d]
        wu32[256 + 64 * d : 256 + 64 * d + M, 0:M] = w
        wu32[256 + 64 * d : 256 + 64 * d + M, 64 : 64 + M] = w
    for f in range(4):
        face = lift[:, f, :]
        for o in range(3):
            w = lax.dot_general(
                turn[o],
                face,
                (((1,), (0,)), ((), ())),
                precision=lax.Precision.HIGHEST,
                preferred_element_type=F32,
            )
            start = 512 + 128 * o + 32 * f
            wu32[start : start + J, 0:M] = w
            wu32[start : start + J, 64 : 64 + M] = w
    u_hi, u_lo = split2(wu32[...])
    wu[:, 0:128] = u_hi
    wu[:, 128:256] = u_lo

    inside = from_inside([first[q, 0:16, :] for q in range(Q)], 0)
    for q in range(Q):
        half[q] = state0[q, 0:16, :] + inside[16 * q : 16 * q + 16]
    inside = from_inside([first[q, 16:32, :] + second[q, 16:32, :] for q in range(Q)], 1)
    for q in range(Q):
        part[q, 16:32, :] = state0[q, 16:32, :] + inside[16 * q : 16 * q + 16]

    near1[...] = near1[...] + arrived(started, recv1)
    outside = from_neighbours(
        lambda f, k: near1[32 * f : 32 * f + 16, 128 * k : 128 * k + 128], 0
    )
    for q in range(Q):
        x = half[q] + outside[16 * q : 16 * q + 16]
        x = jnp.where(is_fine, x, state0[q, 0:16, :])
        half[q] = x
        term[q, 0:16, :] = x
        later[q, 0:16, :] = early[0] * x
        later[q, 16:32, :] = second[q, 16:32, :]
    predict(16, 1, [(later, early)])
    for q in range(Q):
        later[q, 0:16, :] = jnp.where(is_fine, later[q, 0:16, :], second[q, 0:16, :])

    make_table(later)
    started = exchange(send2, recv2, 1)

    for f in range(4):
        top = slice(32 * f, 32 * f + 16)
        for k in range(3):
            lanes = slice(128 * k, 128 * k + 128)
            near1[top, lanes] = jnp.where(is_fine, 0.0, near1[top, lanes])
    near1[...] = near1[...] + dot(gather_loc[...], rhs[...])
    inside = from_inside(
        [
            jnp.where(is_fine, later[q, 0:16, :], first[q, 0:16, :] + second[q, 0:16, :])
            for q in range(Q)
        ],
        0,
    )
    for q in range(Q):
        part[q, 0:16, :] = half[q] + inside[16 * q : 16 * q + 16]
    wait(18)
    unperm = dot_nt(flag(iota((32, 32), 0) == iota((32, 32), 1)).astype(BF16), perm).astype(BF16)
    unperm3 = jnp.concatenate([unperm, unperm, unperm], axis=1)
    offset = (fault * n_off + off) * E
    source_hot = flag(iota((32, 16), 0) + offset == src_elem[...]).astype(BF16)
    source_hot3 = jnp.concatenate([source_hot] * 3, axis=1)

    near1[...] = near1[...] + arrived(started, recv2)
    for h in range(2):
        outside = from_neighbours(
            lambda f, k: near1[
                32 * f + 16 * h : 32 * f + 16 * h + 16, 128 * k : 128 * k + 128
            ],
            h,
        )
        for q in range(Q):
            rows = slice(16 * h, 16 * h + 16)
            part[q, rows, :] = part[q, rows, :] + outside[16 * q : 16 * q + 16]
    hot_ref[:, 0:96] = unperm3
    hot_ref[:, 96:144] = source_hot3


def finish(part, hot, src_term, out_ref):
    for q in range(Q):
        terms = [*split3(part[q][:, 0:M]), *split3(src_term[q])]
        out_ref[q] = dot(hot[...], jnp.concatenate(terms, axis=0))


def on_device(
    modal_state,
    star_mats,
    flux_local,
    flux_nbr,
    stiff_time,
    stiff_vol,
    flux_minus,
    face_proj,
    face_turn,
    face_lift,
    cluster,
    send_elem,
    send_face,
    nbr_index,
    orientation,
    source_elem,
    source_term,
):
    n_fault = lax.axis_size("fault")
    n_off = lax.axis_size("off")
    inputs = [
        jnp.transpose(modal_state, (0, 2, 1)),
        jnp.transpose(star_mats, (1, 2, 0, 3)).reshape(81, 3, E),
        jnp.transpose(flux_local, (1, 2, 0, 3)).reshape(81, 4, E),
        jnp.transpose(flux_nbr, (1, 2, 0, 3)).reshape(81, 4, E),
        stiff_time,
        stiff_vol,
        flux_minus,
        jnp.transpose(face_proj, (2, 0, 1)),
        face_turn,
        jnp.transpose(face_lift, (1, 0, 2)),
        cluster.reshape(1, E),
        send_elem.reshape(1, 72),
        send_face.reshape(1, 72),
        nbr_index,
        orientation,
        source_elem.reshape(1, 16),
        *spread_tables(),
    ]
    own = {1: (84, 8, E), 2: (84, 8, E), 3: (84, 8, E)}
    held = [pltpu.VMEM(own.get(i, x.shape), x.dtype) for i, x in enumerate(inputs)]
    scratch = [
        *held,
        pltpu.VMEM((4, 21, E, 256), F32),
        pltpu.VMEM((Q, 5, E, 128), F32),
        pltpu.VMEM((4, 21, E, 256), F32),
        pltpu.VMEM((4, 21, E, 128), F32),
        pltpu.VMEM((21 * E, 256), BF16),
        pltpu.VMEM((256, 128), F32),
        pltpu.VMEM((256, 256), BF16),
        pltpu.VMEM((2, 144, 256), BF16),
        pltpu.VMEM((2, 144, 256), BF16),
        pltpu.VMEM((896, 128), F32),
        pltpu.VMEM((896, 256), BF16),
        pltpu.VMEM((512, 256), F32),
        pltpu.VMEM((256, 512), BF16),
        pltpu.VMEM((256, 512), BF16),
        pltpu.VMEM((Q, E, 128), F32),
        pltpu.VMEM((Q, E, 128), F32),
        pltpu.VMEM((Q, E, 128), F32),
        pltpu.VMEM((Q, E, 128), F32),
        pltpu.VMEM((Q, FINE, 128), F32),
        pltpu.VMEM((Q, E, 128), F32),
        pltpu.VMEM((128, 384), F32),
        pltpu.VMEM((128, 256), BF16),
        pltpu.VMEM((128, 256), BF16),
        pltpu.VMEM((96, 256), BF16),
        pltpu.VMEM((256, 384), BF16),
        pltpu.VMEM((288, 128), F32),
        pltpu.VMEM((288, 128), F32),
        pltpu.VMEM((6, 48, 128), F32),
        pltpu.VMEM((6, 48, 128), F32),
        pltpu.SemaphoreType.DMA((len(inputs),)),
        pltpu.SemaphoreType.DMA((2, 5)),
        pltpu.SemaphoreType.DMA((2, 5)),
    ]
    part, hot = pl.pallas_call(
        functools.partial(kernel, n_fault, n_off),
        out_shape=[
            jax.ShapeDtypeStruct((Q, E, 128), F32),
            jax.ShapeDtypeStruct((E, 144), BF16),
        ],
        in_specs=[pl.BlockSpec(memory_space=pl.ANY)] * len(inputs),
        out_specs=[pl.BlockSpec(memory_space=pltpu.VMEM)] * 2,
        scratch_shapes=scratch,
        compiler_params=pltpu.CompilerParams(
            collective_id=0, has_side_effects=True, vmem_limit_bytes=56 << 20
        ),
    )(*inputs)
    made = pl.pallas_call(
        finish,
        out_shape=jax.ShapeDtypeStruct((Q, E, M), F32),
        in_specs=[pl.BlockSpec(memory_space=pltpu.VMEM)] * 3,
        out_specs=pl.BlockSpec(memory_space=pltpu.VMEM),
    )(part, hot, jnp.transpose(source_term, (1, 0, 2)))
    return jnp.transpose(made, (0, 2, 1))


def solution(mesh):
    in_specs = (
        P(None, None, ("fault", "off")),
        P(None, None, None, ("fault", "off")),
        P(None, None, None, ("fault", "off")),
        P(None, None, None, ("fault", "off")),
        P(),
        P(),
        P(),
        P(),
        P(),
        P(),
        P(("fault", "off")),
        P("fault", "off", None),
        P("fault", "off", None),
        P(None, ("fault", "off")),
        P(None, ("fault", "off")),
        P(),
        P(),
    )
    out_specs = P(None, None, ("fault", "off"))
    return jax.shard_map(
        on_device, mesh=mesh, in_specs=in_specs, out_specs=out_specs, check_vma=False
    )
```
